32 devices in a mesh: seq: 8 (over z, y), ch: 4 (over x, core).
Axes of the slice: x: 2, y: 2, z: 4, core: 2. Of those that a mesh axis runs over, the one named last changes fastest.
Arguments:
- tokens: bfloat16 [1024, 4096], P('seq', 'ch'), may hold values from -6 to 6
- norm_gain: float32 [4096], replicated, may hold values from 0.5 to 1.5
- in_proj: bfloat16 [4096, 2, 8192], P('seq', None, 'ch'), may hold values from -0.09375 to 0.09375
- conv_weight: float32 [4, 8192], P(None, 'ch'), may hold values from -3 to 3
- conv_bias: float32 [8192], P('ch'), may hold values from -2 to 2
- x_proj: bfloat16 [8192, 544], P('ch'), may hold values from -0.0625 to 0.0625
- dt_proj: bfloat16 [512, 8192], P(None, 'ch'), may hold values from -0.25 to 0.25
- dt_bias: float32 [8192], P('ch'), may hold values from -4 to 1
- a_log: float32 [8192, 16], P('ch'), as said below
- d_skip: float32 [8192], P('ch'), may hold values from -32 to 32
- out_proj: bfloat16 [8192, 4096], P('ch', 'seq'), may hold values from -0.0625 to 0.0625
Outputs:
- mixed: bfloat16 [1024, 4096], P('seq', 'ch')
The draws below stay inside these ranges and needn't reach their ends.
Inputs may be any that keep to these rules, and one draw needn't show every extreme that they name: Every entry of a_log lies between ln(0.2 / 1024) and ln(0.2).
All inputs are finite; a program needn't handle non-finite values.
Results may differ from the reference program's by a relative error of at most 0.014.
Values may be sent and summed in bfloat16 or wider, within the bound.
A program may use at most 128 MiB of HBM per device.

```python
import math
import jax
import jax.numpy as jnp
from jax import lax

D = 4096
E = 8192
R = 512
N = 16
TOKENS = 1024
N_CH = 4


def draw_a_log(key, part):
    key_kind, key_place = jax.random.split(jax.random.fold_in(key, 17))
    share = 0.5
    chosen = jax.random.uniform(key_kind, (E, N), jnp.float32) < share
    where_in = jax.random.uniform(key_place, (E, N), jnp.float32)
    lowest = math.log(0.2 / TOKENS)
    middle = math.log(1.0 / TOKENS)
    highest = math.log(0.2)
    slower = lowest + where_in * (middle - lowest)
    faster = middle + where_in * (highest - middle)
    return jnp.where(chosen, slower, faster).astype(jnp.float32)


def draw_d_skip(key, part):
    key_size = jax.random.fold_in(jax.random.fold_in(key, 29), 0)
    where_in = jax.random.uniform(key_size, (E,), jnp.float32)
    values = 0.5 + where_in
    return values.astype(jnp.float32)


def block_scale(stream_key, shape, cuts, least, largest):
    def one(dim, blocks):
        draws = jax.random.uniform(jax.random.fold_in(jax.random.fold_in(stream_key, 6), dim), (blocks,), jnp.float32, least / len(cuts), largest / len(cuts))
        return jnp.repeat(jnp.exp(draws), shape[dim] // blocks).reshape((-1,) + (1,) * (len(shape) - dim - 1))

    level = one(*cuts[0])
    for cut in cuts[1:]:
        level = level * one(*cut)
    return level


def scatter_about(stream_key, extent, width, reach, cuts=(), held_as=jnp.bfloat16):
    factor_of = block_scale(stream_key, extent, cuts, -0.22, 0.18) if cuts else 1.0
    entries = jax.random.normal(stream_key, extent, jnp.float32) * width * factor_of
    return jnp.minimum(jnp.maximum(entries, -reach), reach).astype(held_as)


def setup_inputs(seed: int = 0) -> dict:
    key_of = jax.random.split(jax.random.key(seed), 12)
    return {
        "tokens": scatter_about(key_of[0], (TOKENS, D), 1.0, 6.0, ((0, 8), (1, 4))),
        "norm_gain": jnp.clip(1.0 + 0.1 * jax.random.normal(key_of[1], (D,), jnp.float32), 0.5, 1.5),
        "in_proj": scatter_about(key_of[2], (D, 2, E), D ** -0.5, 0.09375, ((0, 8), (2, 4))),
        "conv_weight": scatter_about(key_of[3], (4, E), 0.5, 3.0, ((1, 4),), jnp.float32),
        "conv_bias": scatter_about(key_of[4], (E,), 0.3, 2.0, ((0, 4),), jnp.float32),
        "x_proj": scatter_about(key_of[5], (E, R + 2 * N), E ** -0.5, 0.0625, ((0, 4),)),
        "dt_proj": scatter_about(key_of[6], (R, E), R ** -0.5, 0.25, ((1, 4),)),
        "dt_bias": jnp.clip(-4.0 + 5.0 * jax.random.uniform(key_of[7], (E,), jnp.float32) ** block_scale(key_of[7], (E,), ((0, 4),), -0.2, 0.2), -4.0, 1.0),
        "a_log": draw_a_log(jax.random.fold_in(key_of[11], 71), 0),
        "d_skip": draw_d_skip(jax.random.fold_in(key_of[11], 71), 0),
        "out_proj": scatter_about(key_of[10], (E, D), E ** -0.5, 0.0625, ((0, 4), (1, 8))),
    }


def reference(tokens, norm_gain, in_proj, conv_weight, conv_bias, x_proj, dt_proj, dt_bias, a_log, d_skip, out_proj):
    tokens_wide = tokens.astype(jnp.float32)
    scale_rows = lax.rsqrt(lax.optimization_barrier(jnp.mean(tokens_wide * tokens_wide, axis=-1, keepdims=True)) + 1e-06)
    normed = (tokens_wide * scale_rows * norm_gain).astype(jnp.bfloat16)
    both = jnp.dot(normed, in_proj.reshape(D, 2 * E), preferred_element_type=jnp.float32)
    conv_input = both[:, :E].astype(jnp.bfloat16)
    gate = both[:, E:].astype(jnp.bfloat16)
    padded = jnp.concatenate([jnp.zeros((3, E), jnp.bfloat16), conv_input], 0).astype(jnp.float32)
    convolved = conv_bias + conv_weight[0] * padded[0:TOKENS]
    for tap in range(1, 4):
        convolved = convolved + conv_weight[tap] * padded[tap:tap + TOKENS]
    activated = jax.nn.silu(convolved)
    features = jnp.dot(activated.astype(jnp.bfloat16), x_proj, preferred_element_type=jnp.float32)
    step_raw = features[:, :R].astype(jnp.bfloat16)
    b_matrix = features[:, R:R + N]
    c_matrix = features[:, R + N:]
    step_size = jax.nn.softplus(jnp.dot(step_raw, dt_proj, preferred_element_type=jnp.float32) + dt_bias)
    a_matrix = -jnp.exp(a_log)

    def advance(state, inputs):
        step_now, act_now, b_now, c_now = inputs
        state = jnp.exp(step_now[:, None] * a_matrix) * state + (step_now * act_now)[:, None] * b_now[None, :]
        return (state, lax.optimization_barrier(jnp.sum(state * c_now[None, :], axis=1)))
    _, outputs_ssm = lax.scan(advance, jnp.zeros((E, N), jnp.float32), (step_size, activated, b_matrix, c_matrix))
    scanned = outputs_ssm + d_skip * activated
    gated = (scanned * jax.nn.silu(gate.astype(jnp.float32))).astype(jnp.bfloat16)
    group_width = E // N_CH
    running = jnp.zeros((TOKENS, D), jnp.float32)
    for group in range(N_CH):
        partial_value = jnp.dot(gated[:, group * group_width:(group + 1) * group_width], out_proj[group * group_width:(group + 1) * group_width], preferred_element_type=jnp.float32).astype(jnp.bfloat16)
        partial_value = lax.optimization_barrier(partial_value)
        running = running + partial_value.astype(jnp.float32)
    return running.astype(jnp.bfloat16)
```

```python
import functools
import math

import jax
import jax.numpy as jnp
from jax import lax
from jax.experimental import pallas as pl
from jax.experimental.pallas import tpu as pltpu
from jax.sharding import PartitionSpec as P

TAPS = 4
CHUNK = 128


def scan_kernel(
    conv_input,
    gate,
    step_raw,
    b_rows,
    c_rows,
    conv_weight,
    conv_bias,
    dt_proj,
    dt_bias,
    a_log,
    d_skip,
    gated,
    padded,
    step_buf,
    drive_buf,
    part_buf,
    state,
):
    tokens, width = gated.shape
    states = a_log.shape[0]
    chunk = min(CHUNK, tokens)
    padded[0:8] = jnp.zeros((8, width), jnp.float32)
    state[...] = jnp.zeros_like(state)
    a_scaled = jnp.exp(a_log[...]) * (-1.0 / math.log(2.0))

    def one_chunk(index, _):
        rows = pl.ds(pl.multiple_of(index * chunk, chunk), chunk)
        padded[8 : 8 + chunk] = conv_input[rows, :].astype(jnp.float32)
        convolved = conv_bias[...]
        for tap in range(TAPS):
            start = 8 - (TAPS - 1) + tap
            convolved = convolved + conv_weight[tap : tap + 1, :] * padded[start : start + chunk]
        padded[0:8] = padded[chunk : chunk + 8]
        activated = convolved / (1.0 + jnp.exp(-convolved))
        raw = (
            jnp.dot(step_raw[rows, :], dt_proj[...], preferred_element_type=jnp.float32)
            + dt_bias[...]
        )
        step = jnp.maximum(raw, 0.0) + jnp.log1p(jnp.exp(-jnp.abs(raw)))
        step_buf[...] = step
        drive_buf[...] = step * activated
        b_tile = b_rows[:, rows]
        c_tile = c_rows[:, rows]
        now = state[...]
        for t in range(chunk):
            decay = jnp.exp2(step_buf[t : t + 1, :] * a_scaled)
            now = decay * now + drive_buf[t : t + 1, :] * b_tile[:, t : t + 1]
            seen = now * c_tile[:, t : t + 1]
            total = seen[0:8]
            for block in range(1, states // 8):
                total = total + seen[8 * block : 8 * block + 8]
            part_buf[t] = total
        state[...] = now
        scanned = jnp.sum(part_buf[...], axis=1) + d_skip[...] * activated
        gate_now = gate[rows, :].astype(jnp.float32)
        gated[rows, :] = (scanned * (gate_now / (1.0 + jnp.exp(-gate_now)))).astype(gated.dtype)
        return 0

    lax.fori_loop(0, tokens // chunk, one_chunk, 0)


def run_scan(conv_input, *rest):
    tokens, width = conv_input.shape
    chunk = min(CHUNK, tokens)
    states = rest[-2].shape[0]
    vmem = pl.BlockSpec(memory_space=pltpu.VMEM)
    return pl.pallas_call(
        scan_kernel,
        out_shape=jax.ShapeDtypeStruct((tokens, width), jnp.bfloat16),
        in_specs=[vmem] * (1 + len(rest)),
        out_specs=vmem,
        scratch_shapes=[
            pltpu.VMEM((chunk + 8, width), jnp.float32),
            pltpu.VMEM((chunk, width), jnp.float32),
            pltpu.VMEM((chunk, width), jnp.float32),
            pltpu.VMEM((chunk, 8, width), jnp.float32),
            pltpu.VMEM((states, width), jnp.float32),
        ],
        compiler_params=pltpu.CompilerParams(vmem_limit_bytes=40 * 1024 * 1024),
    )(conv_input, *rest)


def on_device(
    tokens,
    norm_gain,
    in_proj,
    conv_weight,
    conv_bias,
    x_proj,
    dt_proj,
    dt_bias,
    a_log,
    d_skip,
    out_proj,
):
    n_seq, n_ch = lax.axis_size("seq"), lax.axis_size("ch")
    seq = lax.axis_index("seq")
    local_tokens = tokens.shape[0]
    all_tokens = local_tokens * n_seq
    channels = in_proj.shape[2]
    width = channels // n_seq
    rank = dt_proj.shape[0]
    states = a_log.shape[1]

    token_rows = lax.all_gather(tokens, "ch", axis=1, tiled=True)
    tokens_wide = token_rows.astype(jnp.float32)
    scale_rows = lax.rsqrt(jnp.mean(tokens_wide * tokens_wide, axis=-1, keepdims=True) + 1e-06)
    normed = (tokens_wide * scale_rows * norm_gain).astype(jnp.bfloat16)
    columns = lax.all_to_all(normed, "seq", split_axis=1, concat_axis=0, tiled=True)

    conv_part = jnp.dot(
        columns, in_proj[:, 0, :], preferred_element_type=jnp.float32
    ).astype(jnp.bfloat16)
    conv_tokens = lax.psum_scatter(conv_part, "seq", scatter_dimension=0, tiled=True)
    gate_part = jnp.einsum(
        "td,dse->ste",
        columns,
        in_proj[:, 1, :].reshape(-1, n_seq, width),
        preferred_element_type=jnp.float32,
    ).astype(jnp.bfloat16)
    gate = lax.psum_scatter(gate_part, "seq", scatter_dimension=0, tiled=False)

    conv_columns = lax.all_to_all(conv_tokens, "seq", split_axis=1, concat_axis=0, tiled=True)
    earlier = lax.ppermute(
        conv_tokens[-(TAPS - 1) :], "seq", [(i, i + 1) for i in range(n_seq - 1)]
    )
    padded = jnp.concatenate([earlier, conv_tokens], 0).astype(jnp.float32)
    convolved = conv_bias
    for tap in range(TAPS):
        convolved = convolved + conv_weight[tap] * padded[tap : tap + local_tokens]
    activated_half = jax.nn.silu(convolved).astype(jnp.bfloat16)
    features = lax.psum(
        jnp.dot(activated_half, x_proj, preferred_element_type=jnp.float32), "ch"
    )
    tail = features[:, rank:]
    high = lax.reduce_precision(tail, 8, 7)
    sent = jnp.concatenate([features[:, :rank], high, tail - high], 1).astype(jnp.bfloat16)
    everyone = lax.all_gather(sent, "seq", axis=0, tiled=True)
    step_raw = everyone[:, :rank]
    pair = everyone[:, rank:].astype(jnp.float32)
    bc_rows = (pair[:, : 2 * states] + pair[:, 2 * states :]).T

    def mine(array, axis):
        return lax.dynamic_slice_in_dim(array, seq * width, width, axis)

    gated = run_scan(
        conv_columns,
        gate,
        step_raw,
        bc_rows[:states],
        bc_rows[states:],
        mine(conv_weight, 1),
        mine(conv_bias, 0)[None],
        mine(dt_proj, 1),
        mine(dt_bias, 0)[None],
        mine(a_log, 0).T,
        mine(d_skip, 0)[None],
    )
    gated_all = lax.all_gather(gated, "seq", axis=1, tiled=True)
    partial_out = jnp.dot(gated_all, out_proj, preferred_element_type=jnp.float32).astype(
        jnp.bfloat16
    )
    summed = lax.psum_scatter(partial_out, "ch", scatter_dimension=0, tiled=True)
    share = n_seq // n_ch
    out_width = out_proj.shape[1]
    blocks = summed.reshape(share, local_tokens, out_width)
    mixed = jnp.zeros((local_tokens, share, out_width), jnp.bfloat16)
    for turn in range(share):
        route = [
            (s * n_ch + c, (share * c + (s + turn) % share) * n_ch + s // share)
            for s in range(n_seq)
            for c in range(n_ch)
        ]
        block = lax.dynamic_index_in_dim(blocks, (seq + turn) % share, 0, keepdims=False)
        arrived = lax.ppermute(block, ("seq", "ch"), route)
        mixed = lax.dynamic_update_slice_in_dim(
            mixed, arrived[:, None], (seq - turn + share) % share, 1
        )
    return mixed.reshape(local_tokens, share * out_width)


def solution(mesh):
    placed = (
        P("seq", "ch"),
        P(),
        P("seq", None, "ch"),
        P(None, "ch"),
        P("ch"),
        P("ch", None),
        P(None, "ch"),
        P("ch"),
        P("ch", None),
        P("ch"),
        P("ch", "seq"),
    )
    return jax.shard_map(
        on_device, mesh=mesh, in_specs=placed, out_specs=P("seq", "ch"), check_vma=False
    )
```

```python
import functools
import math

import jax
import jax.numpy as jnp
from jax import lax
from jax.experimental import pallas as pl
from jax.experimental.pallas import tpu as pltpu
from jax.sharding import PartitionSpec as P

TAPS = 4
CHUNK = 128


def scan_kernel(
    conv_input,
    gate,
    step_raw,
    b_rows,
    c_rows,
    conv_weight,
    conv_bias,
    dt_proj,
    dt_bias,
    a_log,
    d_skip,
    gated,
    padded,
    step_buf,
    drive_buf,
    part_buf,
    state,
):
    tokens, width = gated.shape
    states = a_log.shape[0]
    chunk = min(CHUNK, tokens)
    padded[0:8] = jnp.zeros((8, width), jnp.float32)
    state[...] = jnp.zeros_like(state)
    a_scaled = jnp.exp(a_log[...]) * (-1.0 / math.log(2.0))

    def one_chunk(index, _):
        rows = pl.ds(pl.multiple_of(index * chunk, chunk), chunk)
        padded[8 : 8 + chunk] = conv_input[rows, :].astype(jnp.float32)
        convolved = conv_bias[...]
        for tap in range(TAPS):
            start = 8 - (TAPS - 1) + tap
            convolved = convolved + conv_weight[tap : tap + 1, :] * padded[start : start + chunk]
        padded[0:8] = padded[chunk : chunk + 8]
        activated = convolved / (1.0 + jnp.exp(-convolved))
        raw = (
            jnp.dot(step_raw[rows, :], dt_proj[...], preferred_element_type=jnp.float32)
            + dt_bias[...]
        )
        step = jnp.maximum(raw, 0.0) + jnp.log1p(jnp.exp(-jnp.abs(raw)))
        step_buf[...] = step
        drive_buf[...] = step * activated
        b_tile = b_rows[:, rows]
        c_tile = c_rows[:, rows]
        now = state[...]
        for t in range(chunk):
            decay = jnp.exp2(step_buf[t : t + 1, :] * a_scaled)
            now = decay * now + drive_buf[t : t + 1, :] * b_tile[:, t : t + 1]
            seen = now * c_tile[:, t : t + 1]
            total = seen[0:8]
            for block in range(1, states // 8):
                total = total + seen[8 * block : 8 * block + 8]
            part_buf[t] = total
        state[...] = now
        scanned = jnp.sum(part_buf[...], axis=1) + d_skip[...] * activated
        gate_now = gate[rows, :].astype(jnp.float32)
        gated[rows, :] = (scanned * (gate_now / (1.0 + jnp.exp(-gate_now)))).astype(gated.dtype)
        return 0

    lax.fori_loop(0, tokens // chunk, one_chunk, 0)


def run_scan(conv_input, *rest):
    tokens, width = conv_input.shape
    chunk = min(CHUNK, tokens)
    states = rest[-2].shape[0]
    vmem = pl.BlockSpec(memory_space=pltpu.VMEM)
    return pl.pallas_call(
        scan_kernel,
        out_shape=jax.ShapeDtypeStruct((tokens, width), jnp.bfloat16),
        in_specs=[vmem] * (1 + len(rest)),
        out_specs=vmem,
        scratch_shapes=[
            pltpu.VMEM((chunk + 8, width), jnp.float32),
            pltpu.VMEM((chunk, width), jnp.float32),
            pltpu.VMEM((chunk, width), jnp.float32),
            pltpu.VMEM((chunk, 8, width), jnp.float32),
            pltpu.VMEM((states, width), jnp.float32),
        ],
        compiler_params=pltpu.CompilerParams(vmem_limit_bytes=40 * 1024 * 1024),
    )(conv_input, *rest)


def ring_place(n):
    me = lax.axis_index("seq")
    along, across = lax.div(me, 2), lax.rem(me, 2)
    place = along + across * (n - 1 - 2 * along)

    def index_at(q):
        q = lax.rem(q, n)
        far = lax.div(q, n // 2)
        return 2 * (q + far * (n - 1 - 2 * q)) + far

    return place, index_at


def greet(targets):
    barrier = pltpu.get_barrier_semaphore()
    for target in targets:
        pl.semaphore_signal(
            barrier, inc=1, device_id={"seq": target}, device_id_type=pl.DeviceIdType.MESH
        )
    pl.semaphore_wait(barrier, len(targets))


def push(slots, way, step, target, send_sem, recv_sem):
    return pltpu.make_async_remote_copy(
        src_ref=slots.at[way, step],
        dst_ref=slots.at[way, step + 1],
        send_sem=send_sem.at[way, step],
        recv_sem=recv_sem.at[way, step],
        device_id={"seq": target},
        device_id_type=pl.DeviceIdType.MESH,
    )


def project_kernel(
    n,
    columns,
    w_conv,
    w_gate,
    conv_out,
    gate_out,
    conv_slots,
    gate_slots,
    conv_next,
    gate_next,
    conv_send,
    conv_recv,
    gate_send,
    gate_recv,
):
    place, index_at = ring_place(n)
    targets = (index_at(place + 1), index_at(place + n - 1))
    local, half = conv_slots.shape[2:]
    rows_half = gate_slots.shape[2]
    greet(targets)

    def products(way, q):
        owner = index_at(q)
        rows = pl.ds(pl.multiple_of(owner * local, local), local)
        conv_next[way] = jnp.dot(
            columns[rows, :],
            w_conv[:, way * half : (way + 1) * half],
            preferred_element_type=jnp.float32,
        )
        gate_next[way] = jnp.dot(
            columns[way * rows_half : (way + 1) * rows_half, :],
            w_gate[owner],
            preferred_element_type=jnp.float32,
        )

    for way in range(2):
        products(way, place + (n - 1 if way == 0 else 1))
        conv_slots[way, 0] = conv_next[way].astype(jnp.bfloat16)
        gate_slots[way, 0] = gate_next[way].astype(jnp.bfloat16)

    def turn(step, _):
        copies = []
        for way in range(2):
            copies.append(push(conv_slots, way, step, targets[way], conv_send, conv_recv))
            copies.append(push(gate_slots, way, step, targets[way], gate_send, gate_recv))
        for copy in copies:
            copy.start()
        for way in range(2):
            products(way, place + (2 * n - 2 - step if way == 0 else 2 + step))
        for copy in copies:
            copy.wait()
        for way in range(2):
            conv_slots[way, step + 1] = (
                conv_slots[way, step + 1].astype(jnp.float32) + conv_next[way]
            ).astype(jnp.bfloat16)
            gate_slots[way, step + 1] = (
                gate_slots[way, step + 1].astype(jnp.float32) + gate_next[way]
            ).astype(jnp.bfloat16)
        return 0

    lax.fori_loop(0, n - 1, turn, 0)
    for way in range(2):
        conv_out[:, way * half : (way + 1) * half] = conv_slots[way, n - 1]
        gate_out[way * rows_half : (way + 1) * rows_half, :] = gate_slots[way, n - 1]


def project(columns, w_conv, w_gate):
    n, _, width = w_gate.shape
    total, channels = columns.shape[0], w_conv.shape[1]
    local, half = total // n, channels // 2
    vmem = pl.BlockSpec(memory_space=pltpu.VMEM)
    return pl.pallas_call(
        functools.partial(project_kernel, n),
        out_shape=(
            jax.ShapeDtypeStruct((local, channels), jnp.bfloat16),
            jax.ShapeDtypeStruct((total, width), jnp.bfloat16),
        ),
        in_specs=[vmem] * 3,
        out_specs=(vmem, vmem),
        scratch_shapes=[
            pltpu.VMEM((2, n, local, half), jnp.bfloat16),
            pltpu.VMEM((2, n, total // 2, width), jnp.bfloat16),
            pltpu.VMEM((2, local, half), jnp.float32),
            pltpu.VMEM((2, total // 2, width), jnp.float32),
        ]
        + [pltpu.SemaphoreType.DMA((2, n - 1))] * 4,
        compiler_params=pltpu.CompilerParams(
            collective_id=0, has_side_effects=True, vmem_limit_bytes=56 * 1024 * 1024
        ),
    )(columns, w_conv, w_gate)


def gather_kernel(n, gated, weights, out, slots, totals, send_sem, recv_sem):
    place, index_at = ring_place(n)
    targets = (index_at(place + 1), index_at(place + n - 1))
    rows_half = slots.shape[2]
    greet(targets)

    def add(way, step):
        owner = index_at(place + (n - step if way == 0 else step))
        totals[way] += jnp.dot(
            slots[way, step], weights[owner], preferred_element_type=jnp.float32
        )

    for way in range(2):
        slots[way, 0] = gated[way * rows_half : (way + 1) * rows_half, :]
    totals[...] = jnp.zeros_like(totals)

    def turn(step, _):
        copies = [push(slots, way, step, targets[way], send_sem, recv_sem) for way in range(2)]
        for copy in copies:
            copy.start()
        for way in range(2):
            add(way, step)
        for copy in copies:
            copy.wait()
        return 0

    lax.fori_loop(0, n - 1, turn, 0)
    for way in range(2):
        add(way, n - 1)
        out[way * rows_half : (way + 1) * rows_half, :] = totals[way].astype(out.dtype)


def gather_project(gated, weights):
    n, width, out_width = weights.shape
    total = gated.shape[0]
    vmem = pl.BlockSpec(memory_space=pltpu.VMEM)
    return pl.pallas_call(
        functools.partial(gather_kernel, n),
        out_shape=jax.ShapeDtypeStruct((total, out_width), jnp.bfloat16),
        in_specs=[vmem] * 2,
        out_specs=vmem,
        scratch_shapes=[
            pltpu.VMEM((2, n, total // 2, width), jnp.bfloat16),
            pltpu.VMEM((2, total // 2, out_width), jnp.float32),
            pltpu.SemaphoreType.DMA((2, n - 1)),
            pltpu.SemaphoreType.DMA((2, n - 1)),
        ],
        compiler_params=pltpu.CompilerParams(
            collective_id=1, has_side_effects=True, vmem_limit_bytes=56 * 1024 * 1024
        ),
    )(gated, weights)


def on_device(
    tokens,
    norm_gain,
    in_proj,
    conv_weight,
    conv_bias,
    x_proj,
    dt_proj,
    dt_bias,
    a_log,
    d_skip,
    out_proj,
):
    n_seq, n_ch = lax.axis_size("seq"), lax.axis_size("ch")
    seq = lax.axis_index("seq")
    local_tokens = tokens.shape[0]
    all_tokens = local_tokens * n_seq
    channels = in_proj.shape[2]
    width = channels // n_seq
    rank = dt_proj.shape[0]
    states = a_log.shape[1]

    token_rows = lax.all_gather(tokens, "ch", axis=1, tiled=True)
    tokens_wide = token_rows.astype(jnp.float32)
    scale_rows = lax.rsqrt(jnp.mean(tokens_wide * tokens_wide, axis=-1, keepdims=True) + 1e-06)
    normed = (tokens_wide * scale_rows * norm_gain).astype(jnp.bfloat16)
    columns = lax.all_to_all(normed, "seq", split_axis=1, concat_axis=0, tiled=True)

    w_gate = in_proj[:, 1, :].reshape(-1, n_seq, width).transpose(1, 0, 2)
    conv_tokens, gate = project(columns, in_proj[:, 0, :], w_gate)

    conv_columns = lax.all_to_all(conv_tokens, "seq", split_axis=1, concat_axis=0, tiled=True)
    earlier = lax.ppermute(
        conv_tokens[-(TAPS - 1) :], "seq", [(i, i + 1) for i in range(n_seq - 1)]
    )
    padded = jnp.concatenate([earlier, conv_tokens], 0).astype(jnp.float32)
    convolved = conv_bias
    for tap in range(TAPS):
        convolved = convolved + conv_weight[tap] * padded[tap : tap + local_tokens]
    activated_half = jax.nn.silu(convolved).astype(jnp.bfloat16)
    features = lax.psum(
        jnp.dot(activated_half, x_proj, preferred_element_type=jnp.float32), "ch"
    )
    tail = features[:, rank:]
    high = lax.reduce_precision(tail, 8, 7)
    sent = jnp.concatenate([features[:, :rank], high, tail - high], 1).astype(jnp.bfloat16)
    everyone = lax.all_gather(sent, "seq", axis=0, tiled=True)
    step_raw = everyone[:, :rank]
    pair = everyone[:, rank:].astype(jnp.float32)
    bc_rows = (pair[:, : 2 * states] + pair[:, 2 * states :]).T

    def mine(array, axis):
        return lax.dynamic_slice_in_dim(array, seq * width, width, axis)

    gated = run_scan(
        conv_columns,
        gate,
        step_raw,
        bc_rows[:states],
        bc_rows[states:],
        mine(conv_weight, 1),
        mine(conv_bias, 0)[None],
        mine(dt_proj, 1),
        mine(dt_bias, 0)[None],
        mine(a_log, 0).T,
        mine(d_skip, 0)[None],
    )
    partial_out = gather_project(gated, out_proj.reshape(n_seq, width, -1))
    summed = lax.psum_scatter(partial_out, "ch", scatter_dimension=0, tiled=True)
    share = n_seq // n_ch
    out_width = out_proj.shape[1]
    blocks = summed.reshape(share, local_tokens, out_width)
    mixed = jnp.zeros((local_tokens, share, out_width), jnp.bfloat16)
    for turn in range(share):
        route = [
            (s * n_ch + c, (share * c + (s + turn) % share) * n_ch + s // share)
            for s in range(n_seq)
            for c in range(n_ch)
        ]
        block = lax.dynamic_index_in_dim(blocks, (seq + turn) % share, 0, keepdims=False)
        arrived = lax.ppermute(block, ("seq", "ch"), route)
        mixed = lax.dynamic_update_slice_in_dim(
            mixed, arrived[:, None], (seq - turn + share) % share, 1
        )
    return mixed.reshape(local_tokens, share * out_width)


def solution(mesh):
    placed = (
        P("seq", "ch"),
        P(),
        P("seq", None, "ch"),
        P(None, "ch"),
        P("ch"),
        P("ch", None),
        P(None, "ch"),
        P("ch"),
        P("ch", None),
        P("ch"),
        P("ch", "seq"),
    )
    return jax.shard_map(
        on_device, mesh=mesh, in_specs=placed, out_specs=P("seq", "ch"), check_vma=False
    )
```

```python
import functools
import math

import jax
import jax.numpy as jnp
from jax import lax
from jax.experimental import pallas as pl
from jax.experimental.pallas import tpu as pltpu
from jax.sharding import PartitionSpec as P

TAPS = 4
CHUNK = 128


def scan_kernel(
    conv_input,
    gate,
    step_raw,
    b_rows,
    c_rows,
    conv_weight,
    conv_bias,
    dt_proj,
    dt_bias,
    a_log,
    d_skip,
    gated,
    padded,
    step_buf,
    drive_buf,
    part_buf,
    state,
):
    tokens, width = gated.shape
    states = a_log.shape[0]
    chunk = min(CHUNK, tokens)
    padded[0:8] = jnp.zeros((8, width), jnp.float32)
    state[...] = jnp.zeros_like(state)
    a_scaled = jnp.exp(a_log[...]) * (-1.0 / math.log(2.0))

    def one_chunk(index, _):
        rows = pl.ds(pl.multiple_of(index * chunk, chunk), chunk)
        padded[8 : 8 + chunk] = conv_input[rows, :].astype(jnp.float32)
        convolved = conv_bias[...]
        for tap in range(TAPS):
            start = 8 - (TAPS - 1) + tap
            convolved = convolved + conv_weight[tap : tap + 1, :] * padded[start : start + chunk]
        padded[0:8] = padded[chunk : chunk + 8]
        activated = convolved / (1.0 + jnp.exp(-convolved))
        raw = (
            jnp.dot(step_raw[rows, :], dt_proj[...], preferred_element_type=jnp.float32)
            + dt_bias[...]
        )
        step = jnp.maximum(raw, 0.0) + jnp.log1p(jnp.exp(-jnp.abs(raw)))
        step_buf[...] = step
        drive_buf[...] = step * activated
        b_tile = b_rows[:, rows]
        c_tile = c_rows[:, rows]
        now = state[...]
        for t in range(chunk):
            decay = jnp.exp2(step_buf[t : t + 1, :] * a_scaled)
            now = decay * now + drive_buf[t : t + 1, :] * b_tile[:, t : t + 1]
            seen = now * c_tile[:, t : t + 1]
            total = seen[0:8]
            for block in range(1, states // 8):
                total = total + seen[8 * block : 8 * block + 8]
            part_buf[t] = total
        state[...] = now
        scanned = jnp.sum(part_buf[...], axis=1) + d_skip[...] * activated
        gate_now = gate[rows, :].astype(jnp.float32)
        gated[rows, :] = (scanned * (gate_now / (1.0 + jnp.exp(-gate_now)))).astype(gated.dtype)
        return 0

    lax.fori_loop(0, tokens // chunk, one_chunk, 0)


def run_scan(conv_input, *rest):
    tokens, width = conv_input.shape
    chunk = min(CHUNK, tokens)
    states = rest[-2].shape[0]
    vmem = pl.BlockSpec(memory_space=pltpu.VMEM)
    return pl.pallas_call(
        scan_kernel,
        out_shape=jax.ShapeDtypeStruct((tokens, width), jnp.bfloat16),
        in_specs=[vmem] * (1 + len(rest)),
        out_specs=vmem,
        scratch_shapes=[
            pltpu.VMEM((chunk + 8, width), jnp.float32),
            pltpu.VMEM((chunk, width), jnp.float32),
            pltpu.VMEM((chunk, width), jnp.float32),
            pltpu.VMEM((chunk, 8, width), jnp.float32),
            pltpu.VMEM((states, width), jnp.float32),
        ],
        compiler_params=pltpu.CompilerParams(vmem_limit_bytes=40 * 1024 * 1024),
    )(conv_input, *rest)


def ring_place(n):
    me = lax.axis_index("seq")
    along, across = lax.div(me, 2), lax.rem(me, 2)
    place = along + across * (n - 1 - 2 * along)

    def index_at(q):
        q = lax.rem(q, n)
        far = lax.div(q, n // 2)
        return 2 * (q + far * (n - 1 - 2 * q)) + far

    return place, index_at


def greet(targets):
    barrier = pltpu.get_barrier_semaphore()
    for target in targets:
        pl.semaphore_signal(
            barrier, inc=1, device_id={"seq": target}, device_id_type=pl.DeviceIdType.MESH
        )
    pl.semaphore_wait(barrier, len(targets))


def push(slots, way, step, target, send_sem, recv_sem):
    return pltpu.make_async_remote_copy(
        src_ref=slots.at[way, step],
        dst_ref=slots.at[way, step + 1],
        send_sem=send_sem.at[way, step],
        recv_sem=recv_sem.at[way, step],
        device_id={"seq": target},
        device_id_type=pl.DeviceIdType.MESH,
    )


def project_kernel(
    n,
    columns,
    w_conv,
    w_gate,
    conv_out,
    gate_out,
    conv_slots,
    gate_slots,
    conv_next,
    gate_next,
    conv_send,
    conv_recv,
    gate_send,
    gate_recv,
):
    place, index_at = ring_place(n)
    targets = (index_at(place + 1), index_at(place + n - 1))
    local, half = conv_slots.shape[2:]
    rows_half = gate_slots.shape[2]
    greet(targets)

    def products(way, q):
        owner = index_at(q)
        rows = pl.ds(pl.multiple_of(owner * local, local), local)
        conv_next[way] = jnp.dot(
            columns[rows, :],
            w_conv[:, way * half : (way + 1) * half],
            preferred_element_type=jnp.float32,
        )
        gate_next[way] = jnp.dot(
            columns[way * rows_half : (way + 1) * rows_half, :],
            w_gate[owner],
            preferred_element_type=jnp.float32,
        )

    for way in range(2):
        products(way, place + (n - 1 if way == 0 else 1))
        conv_slots[way, 0] = conv_next[way].astype(jnp.bfloat16)
        gate_slots[way, 0] = gate_next[way].astype(jnp.bfloat16)

    def turn(step, _):
        copies = []
        for way in range(2):
            copies.append(push(conv_slots, way, step, targets[way], conv_send, conv_recv))
            copies.append(push(gate_slots, way, step, targets[way], gate_send, gate_recv))
        for copy in copies:
            copy.start()
        for way in range(2):
            products(way, place + (2 * n - 2 - step if way == 0 else 2 + step))
        for copy in copies:
            copy.wait()
        for way in range(2):
            conv_slots[way, step + 1] = (
                conv_slots[way, step + 1].astype(jnp.float32) + conv_next[way]
            ).astype(jnp.bfloat16)
            gate_slots[way, step + 1] = (
                gate_slots[way, step + 1].astype(jnp.float32) + gate_next[way]
            ).astype(jnp.bfloat16)
        return 0

    lax.fori_loop(0, n - 1, turn, 0)
    for way in range(2):
        conv_out[:, way * half : (way + 1) * half] = conv_slots[way, n - 1]
        gate_out[way * rows_half : (way + 1) * rows_half, :] = gate_slots[way, n - 1]


def project(columns, w_conv, w_gate):
    n, _, width = w_gate.shape
    total, channels = columns.shape[0], w_conv.shape[1]
    local, half = total // n, channels // 2
    vmem = pl.BlockSpec(memory_space=pltpu.VMEM)
    return pl.pallas_call(
        functools.partial(project_kernel, n),
        out_shape=(
            jax.ShapeDtypeStruct((local, channels), jnp.bfloat16),
            jax.ShapeDtypeStruct((total, width), jnp.bfloat16),
        ),
        in_specs=[vmem] * 3,
        out_specs=(vmem, vmem),
        scratch_shapes=[
            pltpu.VMEM((2, n, local, half), jnp.bfloat16),
            pltpu.VMEM((2, n, total // 2, width), jnp.bfloat16),
            pltpu.VMEM((2, local, half), jnp.float32),
            pltpu.VMEM((2, total // 2, width), jnp.float32),
        ]
        + [pltpu.SemaphoreType.DMA((2, n - 1))] * 4,
        compiler_params=pltpu.CompilerParams(
            collective_id=0, has_side_effects=True, vmem_limit_bytes=56 * 1024 * 1024
        ),
    )(columns, w_conv, w_gate)


def gather_kernel(n, gated, weights, out, slots, totals, send_sem, recv_sem):
    place, index_at = ring_place(n)
    targets = (index_at(place + 1), index_at(place + n - 1))
    rows_half = slots.shape[2]
    greet(targets)

    def add(way, step):
        owner = index_at(place + (n - step if way == 0 else step))
        totals[way] += jnp.dot(
            slots[way, step], weights[owner], preferred_element_type=jnp.float32
        )

    for way in range(2):
        slots[way, 0] = gated[way * rows_half : (way + 1) * rows_half, :]
    totals[...] = jnp.zeros_like(totals)

    def turn(step, _):
        copies = [push(slots, way, step, targets[way], send_sem, recv_sem) for way in range(2)]
        for copy in copies:
            copy.start()
        for way in range(2):
            add(way, step)
        for copy in copies:
            copy.wait()
        return 0

    lax.fori_loop(0, n - 1, turn, 0)
    for way in range(2):
        add(way, n - 1)
        out[way * rows_half : (way + 1) * rows_half, :] = totals[way].astype(out.dtype)


def gather_project(gated, weights):
    n, width, out_width = weights.shape
    total = gated.shape[0]
    vmem = pl.BlockSpec(memory_space=pltpu.VMEM)
    return pl.pallas_call(
        functools.partial(gather_kernel, n),
        out_shape=jax.ShapeDtypeStruct((total, out_width), jnp.bfloat16),
        in_specs=[vmem] * 2,
        out_specs=vmem,
        scratch_shapes=[
            pltpu.VMEM((2, n, total // 2, width), jnp.bfloat16),
            pltpu.VMEM((2, total // 2, out_width), jnp.float32),
            pltpu.SemaphoreType.DMA((2, n - 1)),
            pltpu.SemaphoreType.DMA((2, n - 1)),
        ],
        compiler_params=pltpu.CompilerParams(
            collective_id=1, has_side_effects=True, vmem_limit_bytes=56 * 1024 * 1024
        ),
    )(gated, weights)


def feature_kernel(
    n,
    m,
    states,
    activated,
    x_proj,
    out,
    part,
    got,
    block,
    slots,
    sum_send,
    sum_recv,
    all_send,
    all_recv,
    ring_send,
    ring_recv,
):
    place, index_at = ring_place(n)
    targets = (index_at(place + 1), index_at(place + n - 1))
    ch = lax.axis_index("ch")
    peers = [lax.rem(ch + k, m) for k in range(1, m)]
    barrier = pltpu.get_barrier_semaphore()
    for axis, others in (("seq", targets), ("ch", peers)):
        for other in others:
            pl.semaphore_signal(
                barrier, inc=1, device_id={axis: other}, device_id_type=pl.DeviceIdType.MESH
            )
    pl.semaphore_wait(barrier, 2 + len(peers))
    rows = block.shape[1]
    rank = x_proj.shape[1] - 2 * states

    for k in range(m):
        owned = pl.ds(pl.multiple_of(k * rows, rows), rows)
        part[k] = jnp.dot(activated[owned, :], x_proj[...], preferred_element_type=jnp.float32)
    copies = [
        pltpu.make_async_remote_copy(
            src_ref=part.at[peer],
            dst_ref=got.at[k],
            send_sem=sum_send.at[k],
            recv_sem=sum_recv.at[k],
            device_id={"ch": peer},
            device_id_type=pl.DeviceIdType.MESH,
        )
        for k, peer in enumerate(peers)
    ]
    for copy in copies:
        copy.start()
    for copy in copies:
        copy.wait()
    total = part[ch]
    for k in range(m - 1):
        total = total + got[k]
    tail = total[:, rank:]
    high = tail.astype(jnp.bfloat16)
    low = (tail - high.astype(jnp.float32)).astype(jnp.bfloat16)
    block[ch] = jnp.concatenate([total[:, :rank].astype(jnp.bfloat16), high, low], axis=1)
    copies = [
        pltpu.make_async_remote_copy(
            src_ref=block.at[ch],
            dst_ref=block.at[ch],
            send_sem=all_send.at[k],
            recv_sem=all_recv.at[k],
            device_id={"ch": peer},
            device_id_type=pl.DeviceIdType.MESH,
        )
        for k, peer in enumerate(peers)
    ]
    for copy in copies:
        copy.start()
    for copy in copies:
        copy.wait()

    half = m // 2
    for way in range(2):
        slots[way, 0] = block[way * half : (way + 1) * half]

    def keep(way, step):
        owner = index_at(place + (n - step if way == 0 else step))
        out[owner, way * half : (way + 1) * half] = slots[way, step]

    def turn(step, _):
        copies = [push(slots, way, step, targets[way], ring_send, ring_recv) for way in range(2)]
        for copy in copies:
            copy.start()
        for way in range(2):
            keep(way, step)
        for copy in copies:
            copy.wait()
        return 0

    lax.fori_loop(0, n - 1, turn, 0)
    for way in range(2):
        keep(way, n - 1)


def gather_features(activated, x_proj, n, m, states):
    rows = activated.shape[0] // m
    inner = x_proj.shape[1]
    wide = inner + 2 * states
    vmem = pl.BlockSpec(memory_space=pltpu.VMEM)
    return pl.pallas_call(
        functools.partial(feature_kernel, n, m, states),
        out_shape=jax.ShapeDtypeStruct((n, m, rows, wide), jnp.bfloat16),
        in_specs=[vmem] * 2,
        out_specs=vmem,
        scratch_shapes=[
            pltpu.VMEM((m, rows, inner), jnp.float32),
            pltpu.VMEM((m - 1, rows, inner), jnp.float32),
            pltpu.VMEM((m, rows, wide), jnp.bfloat16),
            pltpu.VMEM((2, n, m // 2, rows, wide), jnp.bfloat16),
            pltpu.SemaphoreType.DMA((m - 1,)),
            pltpu.SemaphoreType.DMA((m - 1,)),
            pltpu.SemaphoreType.DMA((m - 1,)),
            pltpu.SemaphoreType.DMA((m - 1,)),
            pltpu.SemaphoreType.DMA((2, n - 1)),
            pltpu.SemaphoreType.DMA((2, n - 1)),
        ],
        compiler_params=pltpu.CompilerParams(
            collective_id=2, has_side_effects=True, vmem_limit_bytes=40 * 1024 * 1024
        ),
    )(activated, x_proj)


def on_device(
    tokens,
    norm_gain,
    in_proj,
    conv_weight,
    conv_bias,
    x_proj,
    dt_proj,
    dt_bias,
    a_log,
    d_skip,
    out_proj,
):
    n_seq, n_ch = lax.axis_size("seq"), lax.axis_size("ch")
    seq = lax.axis_index("seq")
    local_tokens = tokens.shape[0]
    all_tokens = local_tokens * n_seq
    channels = in_proj.shape[2]
    width = channels // n_seq
    rank = dt_proj.shape[0]
    states = a_log.shape[1]

    token_rows = lax.all_gather(tokens, "ch", axis=1, tiled=True)
    w_conv = in_proj[:, 0, :]
    w_gate = in_proj[:, 1, :].reshape(-1, n_seq, width).transpose(1, 0, 2)
    token_rows, w_conv, w_gate = lax.optimization_barrier((token_rows, w_conv, w_gate))
    tokens_wide = token_rows.astype(jnp.float32)
    scale_rows = lax.rsqrt(jnp.mean(tokens_wide * tokens_wide, axis=-1, keepdims=True) + 1e-06)
    normed = (tokens_wide * scale_rows * norm_gain).astype(jnp.bfloat16)
    columns = lax.all_to_all(normed, "seq", split_axis=1, concat_axis=0, tiled=True)

    conv_tokens, gate = project(columns, w_conv, w_gate)

    conv_columns = lax.all_to_all(conv_tokens, "seq", split_axis=1, concat_axis=0, tiled=True)
    earlier = lax.ppermute(
        conv_tokens[-(TAPS - 1) :], "seq", [(i, i + 1) for i in range(n_seq - 1)]
    )
    padded = jnp.concatenate([earlier, conv_tokens], 0).astype(jnp.float32)
    convolved = conv_bias
    for tap in range(TAPS):
        convolved = convolved + conv_weight[tap] * padded[tap : tap + local_tokens]
    activated_half = jax.nn.silu(convolved).astype(jnp.bfloat16)
    everyone = gather_features(activated_half, x_proj, n_seq, n_ch, states)
    everyone = everyone.reshape(all_tokens, -1)
    step_raw = everyone[:, :rank]
    pair = everyone[:, rank:].astype(jnp.float32)
    bc_rows = (pair[:, : 2 * states] + pair[:, 2 * states :]).T

    def mine(array, axis):
        return lax.dynamic_slice_in_dim(array, seq * width, width, axis)

    gated = run_scan(
        conv_columns,
        gate,
        step_raw,
        bc_rows[:states],
        bc_rows[states:],
        mine(conv_weight, 1),
        mine(conv_bias, 0)[None],
        mine(dt_proj, 1),
        mine(dt_bias, 0)[None],
        mine(a_log, 0).T,
        mine(d_skip, 0)[None],
    )
    partial_out = gather_project(gated, out_proj.reshape(n_seq, width, -1))
    summed = lax.psum_scatter(partial_out, "ch", scatter_dimension=0, tiled=True)
    share = n_seq // n_ch
    out_width = out_proj.shape[1]
    blocks = summed.reshape(share, local_tokens, out_width)
    mixed = jnp.zeros((local_tokens, share, out_width), jnp.bfloat16)
    for turn in range(share):
        route = [
            (s * n_ch + c, (share * c + (s + turn) % share) * n_ch + s // share)
            for s in range(n_seq)
            for c in range(n_ch)
        ]
        block = lax.dynamic_index_in_dim(blocks, (seq + turn) % share, 0, keepdims=False)
        arrived = lax.ppermute(block, ("seq", "ch"), route)
        mixed = lax.dynamic_update_slice_in_dim(
            mixed, arrived[:, None], (seq - turn + share) % share, 1
        )
    return mixed.reshape(local_tokens, share * out_width)


def solution(mesh):
    placed = (
        P("seq", "ch"),
        P(),
        P("seq", None, "ch"),
        P(None, "ch"),
        P("ch"),
        P("ch", None),
        P(None, "ch"),
        P("ch"),
        P("ch", None),
        P("ch"),
        P("ch", "seq"),
    )
    return jax.shard_map(
        on_device, mesh=mesh, in_specs=placed, out_specs=P("seq", "ch"), check_vma=False
    )
```

```python
import functools
import math

import jax
import jax.numpy as jnp
from jax import lax
from jax.experimental import pallas as pl
from jax.experimental.pallas import tpu as pltpu
from jax.sharding import PartitionSpec as P

TAPS = 4
CHUNK = 128


def scan_kernel(
    conv_input,
    gate,
    step_raw,
    b_rows,
    c_rows,
    conv_weight,
    conv_bias,
    dt_proj,
    dt_bias,
    a_log,
    d_skip,
    gated,
    padded,
    step_buf,
    drive_buf,
    part_buf,
    state,
):
    tokens, width = gated.shape
    states = a_log.shape[0]
    chunk = min(CHUNK, tokens)
    padded[0:8] = jnp.zeros((8, width), jnp.float32)
    state[...] = jnp.zeros_like(state)
    a_scaled = jnp.exp(a_log[...]) * (-1.0 / math.log(2.0))

    def one_chunk(index, _):
        rows = pl.ds(pl.multiple_of(index * chunk, chunk), chunk)
        padded[8 : 8 + chunk] = conv_input[rows, :].astype(jnp.float32)
        convolved = conv_bias[...]
        for tap in range(TAPS):
            start = 8 - (TAPS - 1) + tap
            convolved = convolved + conv_weight[tap : tap + 1, :] * padded[start : start + chunk]
        padded[0:8] = padded[chunk : chunk + 8]
        activated = convolved / (1.0 + jnp.exp(-convolved))
        raw = (
            jnp.dot(step_raw[rows, :], dt_proj[...], preferred_element_type=jnp.float32)
            + dt_bias[...]
        )
        step = jnp.maximum(raw, 0.0) + jnp.log1p(jnp.exp(-jnp.abs(raw)))
        step_buf[...] = step
        drive_buf[...] = step * activated
        b_tile = b_rows[:, rows]
        c_tile = c_rows[:, rows]
        now = state[...]
        for t in range(chunk):
            decay = jnp.exp2(step_buf[t : t + 1, :] * a_scaled)
            now = decay * now + drive_buf[t : t + 1, :] * b_tile[:, t : t + 1]
            seen = now * c_tile[:, t : t + 1]
            total = seen[0:8]
            for block in range(1, states // 8):
                total = total + seen[8 * block : 8 * block + 8]
            part_buf[t] = total
        state[...] = now
        scanned = jnp.sum(part_buf[...], axis=1) + d_skip[...] * activated
        gate_now = gate[rows, :].astype(jnp.float32)
        gated[rows, :] = (scanned * (gate_now / (1.0 + jnp.exp(-gate_now)))).astype(gated.dtype)
        return 0

    lax.fori_loop(0, tokens // chunk, one_chunk, 0)


def run_scan(conv_input, *rest):
    tokens, width = conv_input.shape
    chunk = min(CHUNK, tokens)
    states = rest[-2].shape[0]
    vmem = pl.BlockSpec(memory_space=pltpu.VMEM)
    return pl.pallas_call(
        scan_kernel,
        out_shape=jax.ShapeDtypeStruct((tokens, width), jnp.bfloat16),
        in_specs=[vmem] * (1 + len(rest)),
        out_specs=vmem,
        scratch_shapes=[
            pltpu.VMEM((chunk + 8, width), jnp.float32),
            pltpu.VMEM((chunk, width), jnp.float32),
            pltpu.VMEM((chunk, width), jnp.float32),
            pltpu.VMEM((chunk, 8, width), jnp.float32),
            pltpu.VMEM((states, width), jnp.float32),
        ],
        compiler_params=pltpu.CompilerParams(vmem_limit_bytes=40 * 1024 * 1024),
    )(conv_input, *rest)


def ring_place(n):
    me = lax.axis_index("seq")
    along, across = lax.div(me, 2), lax.rem(me, 2)
    place = along + across * (n - 1 - 2 * along)

    def index_at(q):
        q = lax.rem(q, n)
        far = lax.div(q, n // 2)
        return 2 * (q + far * (n - 1 - 2 * q)) + far

    return place, index_at


def greet(targets):
    barrier = pltpu.get_barrier_semaphore()
    for target in targets:
        pl.semaphore_signal(
            barrier, inc=1, device_id={"seq": target}, device_id_type=pl.DeviceIdType.MESH
        )
    pl.semaphore_wait(barrier, len(targets))


def push(slots, way, step, target, send_sem, recv_sem):
    return pltpu.make_async_remote_copy(
        src_ref=slots.at[way, step],
        dst_ref=slots.at[way, step + 1],
        send_sem=send_sem.at[way, step],
        recv_sem=recv_sem.at[way, step],
        device_id={"seq": target},
        device_id_type=pl.DeviceIdType.MESH,
    )


def project_kernel(
    n,
    columns,
    w_conv,
    w_gate,
    conv_out,
    gate_out,
    conv_slots,
    gate_slots,
    conv_next,
    gate_next,
    conv_send,
    conv_recv,
    gate_send,
    gate_recv,
):
    place, index_at = ring_place(n)
    targets = (index_at(place + 1), index_at(place + n - 1))
    local, half = conv_slots.shape[2:]
    rows_half = gate_slots.shape[2]
    greet(targets)

    def products(way, q):
        owner = index_at(q)
        rows = pl.ds(pl.multiple_of(owner * local, local), local)
        conv_next[way] = jnp.dot(
            columns[rows, :],
            w_conv[:, way * half : (way + 1) * half],
            preferred_element_type=jnp.float32,
        )
        gate_next[way] = jnp.dot(
            columns[way * rows_half : (way + 1) * rows_half, :],
            w_gate[owner],
            preferred_element_type=jnp.float32,
        )

    for way in range(2):
        products(way, place + (n - 1 if way == 0 else 1))
        conv_slots[way, 0] = conv_next[way].astype(jnp.bfloat16)
        gate_slots[way, 0] = gate_next[way].astype(jnp.bfloat16)

    def turn(step, _):
        copies = []
        for way in range(2):
            copies.append(push(conv_slots, way, step, targets[way], conv_send, conv_recv))
            copies.append(push(gate_slots, way, step, targets[way], gate_send, gate_recv))
        for copy in copies:
            copy.start()
        for way in range(2):
            products(way, place + (2 * n - 2 - step if way == 0 else 2 + step))
        for copy in copies:
            copy.wait()
        for way in range(2):
            conv_slots[way, step + 1] = (
                conv_slots[way, step + 1].astype(jnp.float32) + conv_next[way]
            ).astype(jnp.bfloat16)
            gate_slots[way, step + 1] = (
                gate_slots[way, step + 1].astype(jnp.float32) + gate_next[way]
            ).astype(jnp.bfloat16)
        return 0

    lax.fori_loop(0, n - 1, turn, 0)
    for way in range(2):
        conv_out[:, way * half : (way + 1) * half] = conv_slots[way, n - 1]
        gate_out[way * rows_half : (way + 1) * rows_half, :] = gate_slots[way, n - 1]


def project(columns, w_conv, w_gate):
    n, _, width = w_gate.shape
    total, channels = columns.shape[0], w_conv.shape[1]
    local, half = total // n, channels // 2
    vmem = pl.BlockSpec(memory_space=pltpu.VMEM)
    return pl.pallas_call(
        functools.partial(project_kernel, n),
        out_shape=(
            jax.ShapeDtypeStruct((local, channels), jnp.bfloat16),
            jax.ShapeDtypeStruct((total, width), jnp.bfloat16),
        ),
        in_specs=[vmem] * 3,
        out_specs=(vmem, vmem),
        scratch_shapes=[
            pltpu.VMEM((2, n, local, half), jnp.bfloat16),
            pltpu.VMEM((2, n, total // 2, width), jnp.bfloat16),
            pltpu.VMEM((2, local, half), jnp.float32),
            pltpu.VMEM((2, total // 2, width), jnp.float32),
        ]
        + [pltpu.SemaphoreType.DMA((2, n - 1))] * 4,
        compiler_params=pltpu.CompilerParams(
            collective_id=0, has_side_effects=True, vmem_limit_bytes=56 * 1024 * 1024
        ),
    )(columns, w_conv, w_gate)


def gather_kernel(
    n, m, gated, weights, out, slots, totals, parts, got, send_sem, recv_sem, sum_send, sum_recv
):
    place, index_at = ring_place(n)
    targets = (index_at(place + 1), index_at(place + n - 1))
    rows_half = slots.shape[2]
    ch = lax.axis_index("ch")
    peers = [lax.rem(ch + k, m) for k in range(1, m)]
    barrier = pltpu.get_barrier_semaphore()
    for axis, others in (("seq", targets), ("ch", peers)):
        for other in others:
            pl.semaphore_signal(
                barrier, inc=1, device_id={axis: other}, device_id_type=pl.DeviceIdType.MESH
            )
    pl.semaphore_wait(barrier, 2 + len(peers))

    def add(way, step):
        owner = index_at(place + (n - step if way == 0 else step))
        totals[way] += jnp.dot(
            slots[way, step], weights[owner], preferred_element_type=jnp.float32
        )

    for way in range(2):
        slots[way, 0] = gated[way * rows_half : (way + 1) * rows_half, :]
    totals[...] = jnp.zeros_like(totals)

    def turn(step, _):
        copies = [push(slots, way, step, targets[way], send_sem, recv_sem) for way in range(2)]
        for copy in copies:
            copy.start()
        for way in range(2):
            add(way, step)
        for copy in copies:
            copy.wait()
        return 0

    lax.fori_loop(0, n - 1, turn, 0)
    for way in range(2):
        add(way, n - 1)
    rows = out.shape[0]
    half = m // 2
    for k in range(m):
        start = (k % half) * rows
        parts[k] = totals[k // half, start : start + rows, :].astype(parts.dtype)
    copies = [
        pltpu.make_async_remote_copy(
            src_ref=parts.at[peer],
            dst_ref=got.at[k],
            send_sem=sum_send.at[k],
            recv_sem=sum_recv.at[k],
            device_id={"ch": peer},
            device_id_type=pl.DeviceIdType.MESH,
        )
        for k, peer in enumerate(peers)
    ]
    for copy in copies:
        copy.start()
    for copy in copies:
        copy.wait()
    summed = parts[ch].astype(jnp.float32)
    for k in range(m - 1):
        summed = summed + got[k].astype(jnp.float32)
    out[...] = summed.astype(out.dtype)


def gather_project(gated, weights, m):
    n, width, out_width = weights.shape
    total = gated.shape[0]
    vmem = pl.BlockSpec(memory_space=pltpu.VMEM)
    return pl.pallas_call(
        functools.partial(gather_kernel, n, m),
        out_shape=jax.ShapeDtypeStruct((total // m, out_width), jnp.bfloat16),
        in_specs=[vmem] * 2,
        out_specs=vmem,
        scratch_shapes=[
            pltpu.VMEM((2, n, total // 2, width), jnp.bfloat16),
            pltpu.VMEM((2, total // 2, out_width), jnp.float32),
            pltpu.VMEM((m, total // m, out_width), jnp.bfloat16),
            pltpu.VMEM((m - 1, total // m, out_width), jnp.bfloat16),
            pltpu.SemaphoreType.DMA((2, n - 1)),
            pltpu.SemaphoreType.DMA((2, n - 1)),
            pltpu.SemaphoreType.DMA((m - 1,)),
            pltpu.SemaphoreType.DMA((m - 1,)),
        ],
        compiler_params=pltpu.CompilerParams(
            collective_id=1, has_side_effects=True, vmem_limit_bytes=56 * 1024 * 1024
        ),
    )(gated, weights)


def feature_kernel(
    n,
    m,
    states,
    activated,
    x_proj,
    out,
    part,
    got,
    block,
    slots,
    sum_send,
    sum_recv,
    all_send,
    all_recv,
    ring_send,
    ring_recv,
):
    place, index_at = ring_place(n)
    targets = (index_at(place + 1), index_at(place + n - 1))
    ch = lax.axis_index("ch")
    peers = [lax.rem(ch + k, m) for k in range(1, m)]
    barrier = pltpu.get_barrier_semaphore()
    for axis, others in (("seq", targets), ("ch", peers)):
        for other in others:
            pl.semaphore_signal(
                barrier, inc=1, device_id={axis: other}, device_id_type=pl.DeviceIdType.MESH
            )
    pl.semaphore_wait(barrier, 2 + len(peers))
    rows = block.shape[1]
    rank = x_proj.shape[1] - 2 * states

    for k in range(m):
        owned = pl.ds(pl.multiple_of(k * rows, rows), rows)
        part[k] = jnp.dot(activated[owned, :], x_proj[...], preferred_element_type=jnp.float32)
    copies = [
        pltpu.make_async_remote_copy(
            src_ref=part.at[peer],
            dst_ref=got.at[k],
            send_sem=sum_send.at[k],
            recv_sem=sum_recv.at[k],
            device_id={"ch": peer},
            device_id_type=pl.DeviceIdType.MESH,
        )
        for k, peer in enumerate(peers)
    ]
    for copy in copies:
        copy.start()
    for copy in copies:
        copy.wait()
    total = part[ch]
    for k in range(m - 1):
        total = total + got[k]
    tail = total[:, rank:]
    high = tail.astype(jnp.bfloat16)
    low = (tail - high.astype(jnp.float32)).astype(jnp.bfloat16)
    block[ch] = jnp.concatenate([total[:, :rank].astype(jnp.bfloat16), high, low], axis=1)
    copies = [
        pltpu.make_async_remote_copy(
            src_ref=block.at[ch],
            dst_ref=block.at[ch],
            send_sem=all_send.at[k],
            recv_sem=all_recv.at[k],
            device_id={"ch": peer},
            device_id_type=pl.DeviceIdType.MESH,
        )
        for k, peer in enumerate(peers)
    ]
    for copy in copies:
        copy.start()
    for copy in copies:
        copy.wait()

    half = m // 2
    for way in range(2):
        slots[way, 0] = block[way * half : (way + 1) * half]

    def keep(way, step):
        owner = index_at(place + (n - step if way == 0 else step))
        out[owner, way * half : (way + 1) * half] = slots[way, step]

    def turn(step, _):
        copies = [push(slots, way, step, targets[way], ring_send, ring_recv) for way in range(2)]
        for copy in copies:
            copy.start()
        for way in range(2):
            keep(way, step)
        for copy in copies:
            copy.wait()
        return 0

    lax.fori_loop(0, n - 1, turn, 0)
    for way in range(2):
        keep(way, n - 1)


def gather_features(activated, x_proj, n, m, states):
    rows = activated.shape[0] // m
    inner = x_proj.shape[1]
    wide = inner + 2 * states
    vmem = pl.BlockSpec(memory_space=pltpu.VMEM)
    return pl.pallas_call(
        functools.partial(feature_kernel, n, m, states),
        out_shape=jax.ShapeDtypeStruct((n, m, rows, wide), jnp.bfloat16),
        in_specs=[vmem] * 2,
        out_specs=vmem,
        scratch_shapes=[
            pltpu.VMEM((m, rows, inner), jnp.float32),
            pltpu.VMEM((m - 1, rows, inner), jnp.float32),
            pltpu.VMEM((m, rows, wide), jnp.bfloat16),
            pltpu.VMEM((2, n, m // 2, rows, wide), jnp.bfloat16),
            pltpu.SemaphoreType.DMA((m - 1,)),
            pltpu.SemaphoreType.DMA((m - 1,)),
            pltpu.SemaphoreType.DMA((m - 1,)),
            pltpu.SemaphoreType.DMA((m - 1,)),
            pltpu.SemaphoreType.DMA((2, n - 1)),
            pltpu.SemaphoreType.DMA((2, n - 1)),
        ],
        compiler_params=pltpu.CompilerParams(
            collective_id=2, has_side_effects=True, vmem_limit_bytes=40 * 1024 * 1024
        ),
    )(activated, x_proj)


def on_device(
    tokens,
    norm_gain,
    in_proj,
    conv_weight,
    conv_bias,
    x_proj,
    dt_proj,
    dt_bias,
    a_log,
    d_skip,
    out_proj,
):
    n_seq, n_ch = lax.axis_size("seq"), lax.axis_size("ch")
    seq = lax.axis_index("seq")
    local_tokens = tokens.shape[0]
    all_tokens = local_tokens * n_seq
    channels = in_proj.shape[2]
    width = channels // n_seq
    rank = dt_proj.shape[0]
    states = a_log.shape[1]

    token_rows = lax.all_gather(tokens, "ch", axis=1, tiled=True)
    w_conv = in_proj[:, 0, :]
    w_gate = in_proj[:, 1, :].reshape(-1, n_seq, width).transpose(1, 0, 2)
    token_rows, w_conv = lax.optimization_barrier((token_rows, w_conv))
    tokens_wide = token_rows.astype(jnp.float32)
    scale_rows = lax.rsqrt(jnp.mean(tokens_wide * tokens_wide, axis=-1, keepdims=True) + 1e-06)
    normed = (tokens_wide * scale_rows * norm_gain).astype(jnp.bfloat16)
    columns = lax.all_to_all(normed, "seq", split_axis=1, concat_axis=0, tiled=True)

    conv_tokens, gate = project(columns, w_conv, w_gate)

    conv_columns = lax.all_to_all(conv_tokens, "seq", split_axis=1, concat_axis=0, tiled=True)
    earlier = lax.ppermute(
        conv_tokens[-(TAPS - 1) :], "seq", [(i, i + 1) for i in range(n_seq - 1)]
    )
    padded = jnp.concatenate([earlier, conv_tokens], 0).astype(jnp.float32)
    convolved = conv_bias
    for tap in range(TAPS):
        convolved = convolved + conv_weight[tap] * padded[tap : tap + local_tokens]
    activated_half = jax.nn.silu(convolved).astype(jnp.bfloat16)
    everyone = gather_features(activated_half, x_proj, n_seq, n_ch, states)
    everyone = everyone.reshape(all_tokens, -1)
    step_raw = everyone[:, :rank]
    pair = everyone[:, rank:].astype(jnp.float32)
    bc_rows = (pair[:, : 2 * states] + pair[:, 2 * states :]).T

    def mine(array, axis):
        return lax.dynamic_slice_in_dim(array, seq * width, width, axis)

    gated = run_scan(
        conv_columns,
        gate,
        step_raw,
        bc_rows[:states],
        bc_rows[states:],
        mine(conv_weight, 1),
        mine(conv_bias, 0)[None],
        mine(dt_proj, 1),
        mine(dt_bias, 0)[None],
        mine(a_log, 0).T,
        mine(d_skip, 0)[None],
    )
    summed = gather_project(gated, out_proj.reshape(n_seq, width, -1), n_ch)
    share = n_seq // n_ch
    out_width = out_proj.shape[1]
    blocks = summed.reshape(share, local_tokens, out_width)
    mixed = jnp.zeros((local_tokens, share, out_width), jnp.bfloat16)
    for turn in range(share):
        route = [
            (s * n_ch + c, (share * c + (s + turn) % share) * n_ch + s // share)
            for s in range(n_seq)
            for c in range(n_ch)
        ]
        block = lax.dynamic_index_in_dim(blocks, (seq + turn) % share, 0, keepdims=False)
        arrived = lax.ppermute(block, ("seq", "ch"), route)
        mixed = lax.dynamic_update_slice_in_dim(
            mixed, arrived[:, None], (seq - turn + share) % share, 1
        )
    return mixed.reshape(local_tokens, share * out_width)


def solution(mesh):
    placed = (
        P("seq", "ch"),
        P(),
        P("seq", None, "ch"),
        P(None, "ch"),
        P("ch"),
        P("ch", None),
        P(None, "ch"),
        P("ch"),
        P("ch", None),
        P("ch"),
        P("ch", "seq"),
    )
    return jax.shard_map(
        on_device, mesh=mesh, in_specs=placed, out_specs=P("seq", "ch"), check_vma=False
    )
```
